32 devices in a mesh: atom: 16 (over z, y, core), aux: 2 (over x).
Axes of the slice: x: 2, y: 2, z: 4, core: 2. Of those that a mesh axis runs over, the one named last changes fastest.
Arguments:
- three: bfloat16 [32, 128, 128, 384], P('atom', 'aux'), may hold values from -0.5 to 0.5
- occupied: bfloat16 [4096, 384], P(('atom', 'aux')), may hold values from -0.3125 to 0.3125
- virtual: bfloat16 [4096, 384], P(('atom', 'aux')), may hold values from -0.3125 to 0.3125
- three_mask: int32 [32, 3], replicated, may hold values from 0 to 1, as said below
- occ_mask: int32 [32, 3], replicated, may hold values from 0 to 1, as said below
- vir_mask: int32 [32, 3], replicated, may hold values from 0 to 1, as said below
- atom_sizes: int32 [32], replicated, may hold values from 64 to 128
Outputs:
- polarizability: float32 [32, 128, 384], P('atom', 'aux')
The draws below stay inside these ranges and needn't reach their ends.
Inputs may be any that keep to these rules, and one draw needn't show every extreme that they name: three_mask[b, 1] = 1 for every block b; the slab pairs its atom blocks into molecules of two, and every block keeps its tile towards the neighbouring molecule: three_mask[b, 0] = 1 for even b and three_mask[b, 2] = 1 for odd b. occ_mask[b, 1] = 1 for every block b; occ_mask[b, 0] = 1 where b is a multiple of 2, and occ_mask[b, 2] = 1 where b + 1 is a multiple of 2. vir_mask[b, 1] = 1 for every block b.
All inputs are finite; a program needn't handle non-finite values.
Results may differ from the reference program's by a relative error of at most 0.0041.
Values may be sent and summed in bfloat16 or wider, within the bound.
A program may use at most 320 MiB of HBM per device.

```python
import jax
import jax.numpy as jnp
from jax import lax

BLK = 128
AB = 128
A_DEV = 2
NA = 32


def random_mask(key, salt):
    picks = jax.random.randint(jax.random.fold_in(key, salt), (NA, 3), 0, 4)
    kept = (picks < 3).astype(jnp.int32)
    columns = jnp.arange(3, dtype=jnp.int32)[None, :]
    return jnp.where(columns == 1, 1, kept)


def edge_mask(key, salt):
    kept = random_mask(key, salt)
    blocks = jnp.arange(NA, dtype=jnp.int32)[:, None]
    columns = jnp.arange(3, dtype=jnp.int32)[None, :]
    first_edge = (blocks % A_DEV == 0) & (columns == 0)
    last_edge = (blocks % A_DEV == A_DEV - 1) & (columns == 2)
    return jnp.where(first_edge | last_edge, 1, kept)


def draw_three_mask(key, part):
    return edge_mask(key, 101)


def draw_occ_mask(key, part):
    return edge_mask(key, 202)


def draw_vir_mask(key, part):
    return random_mask(key, 303)


def plant(values, key, low, high):
    extent = values.shape
    spot = [jax.random.randint(jax.random.fold_in(key, axis), (), 0, extent[axis]) for axis in range(len(extent))]
    values = values.at[tuple(spot)].set(low)
    longest = extent.index(max(extent))
    spot[longest] = (spot[longest] + 1) % extent[longest]
    return values.at[tuple(spot)].set(high)


def steps_of(stream_key, dims, shards, low, top_value):
    loudness = 1.0
    for position, shards_of in shards:
        draws = jax.random.uniform(jax.random.fold_in(jax.random.fold_in(stream_key, 6), position), (shards_of,), jnp.float32, low / len(shards), top_value / len(shards))
        loudness = loudness * jnp.repeat(jnp.exp(draws), dims[position] // shards_of).reshape((-1,) + (1,) * (len(dims) - 1 - position))
    return loudness


def noise(rng, dims, scale, limit, cuts=(), kind=jnp.bfloat16):
    factor_of = steps_of(rng, dims, cuts, -0.22, 0.18) if cuts else 1.0
    result = jax.random.normal(rng, dims, jnp.float32) * scale * factor_of
    return jnp.minimum(jnp.maximum(result, -limit), limit).astype(kind)


def setup_inputs(seed: int = 0) -> dict:
    seeds = jax.random.split(jax.random.key(seed), 8)
    return {
        "three": noise(seeds[0], (NA, AB, BLK, 3 * BLK), BLK ** -0.5, 0.5, ((0, 16), (1, 2))),
        "occupied": noise(seeds[1], (NA * BLK, 3 * BLK), (3 * BLK) ** -0.5, 0.3125, ((0, 32),)),
        "virtual": noise(seeds[2], (NA * BLK, 3 * BLK), (3 * BLK) ** -0.5, 0.3125, ((0, 32),)),
        "three_mask": draw_three_mask(jax.random.fold_in(seeds[7], 71), 0),
        "occ_mask": draw_occ_mask(jax.random.fold_in(seeds[7], 71), 0),
        "vir_mask": draw_vir_mask(jax.random.fold_in(seeds[7], 71), 0),
        "atom_sizes": plant(jax.random.randint(seeds[6], (NA,), BLK // 2, BLK + 1), jax.random.fold_in(seeds[6], 1), BLK // 2, BLK).astype(jnp.int32),
    }


def band_live(atom_sizes, mask_table, block_width):
    total_blocks = atom_sizes.shape[0]
    inside = jnp.arange(block_width, dtype=jnp.int32)
    blocks = jnp.arange(total_blocks, dtype=jnp.int32)
    partners = (blocks[:, None] + jnp.arange(3, dtype=jnp.int32)[None, :] + total_blocks - 1) % total_blocks
    row_ok = inside[None, :] < atom_sizes[:, None]
    col_ok = inside[None, None, :] < atom_sizes[partners][:, :, None]
    live_blocks = mask_table > 0
    both = row_ok[:, :, None, None] & col_ok[:, None, :, :] & live_blocks[:, None, :, None]
    return both.reshape(total_blocks, block_width, 3 * block_width)


def block_live(mask_table, block_width):
    total_blocks = mask_table.shape[0]
    spread = jnp.broadcast_to((mask_table > 0)[:, None, :, None], (total_blocks, block_width, 3, block_width))
    return spread.reshape(total_blocks, block_width, 3 * block_width)


def reference(three, occupied, virtual, three_mask, occ_mask, vir_mask, atom_sizes):
    zero_bf = jnp.zeros((), jnp.bfloat16)
    band_ok = band_live(atom_sizes, three_mask, BLK)
    occ_live = jnp.where(block_live(occ_mask, BLK), occupied.reshape(NA, BLK, 3 * BLK), zero_bf)
    vir_live = jnp.where(block_live(vir_mask, BLK), virtual.reshape(NA, BLK, 3 * BLK), zero_bf)

    def coupling_of(block):
        return jnp.where(band_ok[block][None], three[block], zero_bf)

    def paired_of(source, target):
        coupled = coupling_of(source).astype(jnp.float32)
        mixed = jnp.zeros((AB, BLK, 5 * BLK), jnp.float32)
        for offset in range(3):
            partner = (source + offset - 1 + NA) % NA
            vir_rows = vir_live[partner].astype(jnp.float32)
            product = jnp.einsum('pab,bc->pac', coupled[:, :, offset * BLK:(offset + 1) * BLK], vir_rows)
            mixed = mixed.at[:, :, offset * BLK:(offset + 3) * BLK].add(product)
        mixed = lax.optimization_barrier(mixed.astype(jnp.bfloat16)).astype(jnp.float32)
        density = occ_live[source][:, target * BLK:(target + 1) * BLK].astype(jnp.float32)
        screened = jnp.einsum('mj,pmc->pjc', density, mixed[:, :, target * BLK:(target + 3) * BLK])
        return lax.optimization_barrier(screened.astype(jnp.bfloat16)).astype(jnp.float32)

    def target_rows(block):
        coupled = coupling_of(block).astype(jnp.float32)
        pieces = []
        for offset in range(3):
            source = (block + offset - 1 + NA) % NA
            paired = paired_of(source, 2 - offset)
            pieces.append(jnp.einsum('qrc,prc->qp', coupled, paired))
        return jnp.concatenate(pieces, axis=1)

    return lax.map(target_rows, jnp.arange(NA, dtype=jnp.int32))
```

```python
import jax
import jax.numpy as jnp
from jax import lax
from jax.sharding import PartitionSpec as P

CHUNKS = (16, 48, 48, 16)


def shift(value, axis, steps):
    count = lax.axis_size(axis)
    pairs = [(source, (source + steps) % count) for source in range(count)]
    return lax.ppermute(value, axis, pairs)


def shards(three, occupied, virtual, three_mask, occ_mask, vir_mask, atom_sizes):
    bf = jnp.bfloat16
    f32 = jnp.float32
    nb, aux_local, width, _ = three.shape
    total = atom_sizes.shape[0]
    first = lax.axis_index("atom") * nb
    side = lax.axis_index("aux")

    bounds = []
    low = 0
    for rows in CHUNKS:
        bounds.append((low, low + rows))
        low += rows
    local = [three[:, :, lo:hi].transpose(0, 2, 1, 3) for lo, hi in bounds]
    both = [lax.all_gather(piece, "aux", axis=0, tiled=False) for piece in local]

    vir_rows = lax.all_gather(virtual, "aux", axis=0, tiled=True)
    occ_rows = lax.all_gather(occupied, "aux", axis=0, tiled=True)
    vir_rows = vir_rows.reshape(nb, width, 3 * width)
    vir_ext = jnp.concatenate(
        [shift(vir_rows[-1:], "atom", 1), vir_rows, shift(vir_rows[:1], "atom", -1)], axis=0
    )

    ids = jnp.arange(total, dtype=jnp.int32)
    near = (ids[:, None] + jnp.arange(-1, 2, dtype=jnp.int32)[None, :] + total) % total
    inside = jnp.arange(width, dtype=jnp.int32)
    fits = inside[None, :] < atom_sizes[:, None]

    def window(table, start, length):
        rolled = jnp.roll(table, -(first + start), axis=0)
        return rolled[:length]

    fits_w = window(fits, -2, nb + 4)
    tm = window(three_mask > 0, -1, nb + 2)
    vm = window(vir_mask > 0, -1, nb + 2)
    om = window(occ_mask > 0, 0, nb)

    bands = []
    densities = []
    for l in range(nb):
        rows = []
        for o in range(3):
            b = l + o
            tile = vir_ext[b].reshape(width, 3, width)
            cols_ok = fits_w[b : b + 3]
            row_ok = fits_w[b + 1] & tm[l + 1, o]
            ok = row_ok[:, None, None] & (cols_ok & vm[b][:, None])[None]
            tile = jnp.where(ok, tile, 0).reshape(width, 3 * width)
            rows.append(jnp.pad(tile, ((0, 0), (o * width, (2 - o) * width))))
        bands.append(jnp.concatenate(rows, axis=0))
        occ = occ_rows[l * width : (l + 1) * width].reshape(width, 3, width)
        targets = fits_w[l + 1 : l + 4]
        ok = fits_w[l + 2][:, None, None] & (targets & om[l][:, None])[None]
        densities.append(jnp.where(ok, occ, 0))
    band = jnp.stack(bands).astype(bf)
    density = jnp.stack(densities).astype(bf)

    mixed = jnp.einsum("lpmb,lbk->lpmk", three, band, preferred_element_type=f32).astype(bf)
    keep = [tm[t : t + nb] for t in range(3)]

    def pair(t):
        out = jnp.einsum(
            "lmj,lpmc->ljpc",
            density[:, :, t],
            mixed[:, :, :, t * width : (t + 3) * width],
            preferred_element_type=f32,
        )
        ok = jnp.repeat(keep[t], width, axis=1)
        return jnp.where(ok[:, None, None, :], out, 0).astype(bf)

    up = pair(2)
    from_left = shift(up[-1:], "atom", 1)
    down = pair(0)
    from_right = shift(down[:1], "atom", -1)
    mid = pair(1)
    before = jnp.concatenate([from_left, up[:-1]], axis=0)
    after = jnp.concatenate([down[1:], from_right], axis=0)
    sources = jnp.stack([before, mid, after], axis=2)

    def contract(pieces):
        acc = None
        for (lo, hi), piece in zip(bounds, pieces):
            part = jnp.einsum(
                "lrqc,lropc->lqop", piece, sources[:, lo:hi], preferred_element_type=f32
            )
            acc = part if acc is None else acc + part
        return acc

    parts = [contract([piece[s] for piece in both]) for s in range(2)]
    own = jnp.where(side == 0, parts[0], parts[1])
    cross = jnp.where(side == 0, parts[1], parts[0])
    got = shift(cross, "aux", 1)
    sides = jnp.where(
        side == 0,
        jnp.concatenate([own, got], axis=3),
        jnp.concatenate([got, own], axis=3),
    )
    return sides.reshape(nb, aux_local, -1)


def solution(mesh):
    in_specs = (
        P("atom", "aux", None, None),
        P(("atom", "aux"), None),
        P(("atom", "aux"), None),
        P(),
        P(),
        P(),
        P(),
    )
    out_specs = P("atom", "aux", None)
    return jax.shard_map(shards, mesh=mesh, in_specs=in_specs, out_specs=out_specs, check_vma=False)
```

```python
import jax
import jax.numpy as jnp
from jax import lax
from jax.sharding import PartitionSpec as P

CHUNKS = (24, 16, 8, 16, 48, 16)


def shift(value, axis, steps):
    count = lax.axis_size(axis)
    pairs = [(source, (source + steps) % count) for source in range(count)]
    return lax.ppermute(value, axis, pairs)


def shards(three, occupied, virtual, three_mask, occ_mask, vir_mask, atom_sizes):
    bf = jnp.bfloat16
    f32 = jnp.float32
    nb, aux_local, width, _ = three.shape
    total = atom_sizes.shape[0]
    first = lax.axis_index("atom") * nb
    side = lax.axis_index("aux")

    bounds = []
    low = 0
    for rows in CHUNKS:
        bounds.append((low, low + rows))
        low += rows
    local = [three[:, :, lo:hi].transpose(0, 2, 1, 3) for lo, hi in bounds]
    remote = []
    for piece in local:
        if remote:
            piece, _ = lax.optimization_barrier((piece, remote[-1]))
        remote.append(shift(piece, "aux", 1))

    vir_rows = lax.all_gather(virtual, "aux", axis=0, tiled=True)
    occ_rows = lax.all_gather(occupied, "aux", axis=0, tiled=True)
    vir_rows = vir_rows.reshape(nb, width, 3 * width)
    vir_ext = jnp.concatenate(
        [shift(vir_rows[-1:], "atom", 1), vir_rows, shift(vir_rows[:1], "atom", -1)], axis=0
    )

    ids = jnp.arange(total, dtype=jnp.int32)
    near = (ids[:, None] + jnp.arange(-1, 2, dtype=jnp.int32)[None, :] + total) % total
    inside = jnp.arange(width, dtype=jnp.int32)
    fits = inside[None, :] < atom_sizes[:, None]

    def window(table, start, length):
        rolled = jnp.roll(table, -(first + start), axis=0)
        return rolled[:length]

    fits_w = window(fits, -2, nb + 4)
    tm = window(three_mask > 0, -1, nb + 2)
    vm = window(vir_mask > 0, -1, nb + 2)
    om = window(occ_mask > 0, 0, nb)

    bands = []
    densities = []
    for l in range(nb):
        rows = []
        for o in range(3):
            b = l + o
            tile = vir_ext[b].reshape(width, 3, width)
            cols_ok = fits_w[b : b + 3]
            row_ok = fits_w[b + 1] & tm[l + 1, o]
            ok = row_ok[:, None, None] & (cols_ok & vm[b][:, None])[None]
            tile = jnp.where(ok, tile, 0).reshape(width, 3 * width)
            rows.append(jnp.pad(tile, ((0, 0), (o * width, (2 - o) * width))))
        bands.append(jnp.concatenate(rows, axis=0))
        occ = occ_rows[l * width : (l + 1) * width].reshape(width, 3, width)
        targets = fits_w[l + 1 : l + 4]
        ok = fits_w[l + 2][:, None, None] & (targets & om[l][:, None])[None]
        densities.append(jnp.where(ok, occ, 0))
    band = jnp.stack(bands).astype(bf)
    density = jnp.stack(densities).astype(bf)

    three, band, _ = lax.optimization_barrier((three, band, remote[0]))
    mixed = jnp.einsum("lpmb,lbk->lpmk", three, band, preferred_element_type=f32).astype(bf)
    keep = [tm[t : t + nb] for t in range(3)]

    def pair(t):
        out = jnp.einsum(
            "lmj,lpmc->ljpc",
            density[:, :, t],
            mixed[:, :, :, t * width : (t + 3) * width],
            preferred_element_type=f32,
        )
        ok = jnp.repeat(keep[t], width, axis=1)
        return jnp.where(ok[:, None, None, :], out, 0).astype(bf)

    mixed, _ = lax.optimization_barrier((mixed, remote[1]))
    up = pair(2)
    from_left = shift(up[-1:], "atom", 1)
    mixed, up, _ = lax.optimization_barrier((mixed, up, remote[2]))
    down = pair(0)
    from_right = shift(down[:1], "atom", -1)
    mixed, down, _ = lax.optimization_barrier((mixed, down, remote[3]))
    mid = pair(1)
    before = jnp.concatenate([from_left, up[:-1]], axis=0)
    after = jnp.concatenate([down[1:], from_right], axis=0)
    sources = jnp.stack([before, mid, after], axis=2)

    def contract(pieces):
        acc = None
        for (lo, hi), piece in zip(bounds, pieces):
            part = jnp.einsum(
                "lrqc,lropc->lqop", piece, sources[:, lo:hi], preferred_element_type=f32
            )
            acc = part if acc is None else acc + part
        return acc

    own = contract(local)
    cross = contract(remote)
    got = shift(cross, "aux", 1)
    sides = jnp.where(
        side == 0,
        jnp.concatenate([own, got], axis=3),
        jnp.concatenate([got, own], axis=3),
    )
    return sides.reshape(nb, aux_local, -1)


def solution(mesh):
    in_specs = (
        P("atom", "aux", None, None),
        P(("atom", "aux"), None),
        P(("atom", "aux"), None),
        P(),
        P(),
        P(),
        P(),
    )
    out_specs = P("atom", "aux", None)
    return jax.shard_map(shards, mesh=mesh, in_specs=in_specs, out_specs=out_specs, check_vma=False)
```

```python
import jax
import jax.numpy as jnp
from jax import lax
from jax.sharding import PartitionSpec as P

CHUNKS = (16, 72)


def shift(value, axis, steps):
    count = lax.axis_size(axis)
    pairs = [(source, (source + steps) % count) for source in range(count)]
    return lax.ppermute(value, axis, pairs)


def shards(three, occupied, virtual, three_mask, occ_mask, vir_mask, atom_sizes):
    bf = jnp.bfloat16
    f32 = jnp.float32
    nb, aux_local, width, _ = three.shape
    total = atom_sizes.shape[0]
    first = lax.axis_index("atom") * nb
    side = lax.axis_index("aux")

    bounds = []
    low = 0
    for rows in CHUNKS:
        bounds.append((low, low + rows))
        low += rows
    local = [three[:, :, lo:hi].transpose(0, 2, 1, 3) for lo, hi in bounds]
    rest = three[:, :, low:].transpose(0, 2, 1, 3)
    rest_other = shift(rest, "aux", 1)
    both = [lax.all_gather(piece, "aux", axis=0, tiled=False) for piece in local]

    vir_rows = lax.all_gather(virtual, "aux", axis=0, tiled=True)
    occ_rows = lax.all_gather(occupied, "aux", axis=0, tiled=True)
    vir_rows = vir_rows.reshape(nb, width, 3 * width)
    vir_ext = jnp.concatenate(
        [shift(vir_rows[-1:], "atom", 1), vir_rows, shift(vir_rows[:1], "atom", -1)], axis=0
    )

    ids = jnp.arange(total, dtype=jnp.int32)
    near = (ids[:, None] + jnp.arange(-1, 2, dtype=jnp.int32)[None, :] + total) % total
    inside = jnp.arange(width, dtype=jnp.int32)
    fits = inside[None, :] < atom_sizes[:, None]

    def window(table, start, length):
        rolled = jnp.roll(table, -(first + start), axis=0)
        return rolled[:length]

    fits_w = window(fits, -2, nb + 4)
    tm = window(three_mask > 0, -1, nb + 2)
    vm = window(vir_mask > 0, -1, nb + 2)
    om = window(occ_mask > 0, 0, nb)

    bands = []
    densities = []
    for l in range(nb):
        rows = []
        for o in range(3):
            b = l + o
            tile = vir_ext[b].reshape(width, 3, width)
            cols_ok = fits_w[b : b + 3]
            row_ok = fits_w[b + 1] & tm[l + 1, o]
            ok = row_ok[:, None, None] & (cols_ok & vm[b][:, None])[None]
            tile = jnp.where(ok, tile, 0).reshape(width, 3 * width)
            rows.append(jnp.pad(tile, ((0, 0), (o * width, (2 - o) * width))))
        bands.append(jnp.concatenate(rows, axis=0))
        occ = occ_rows[l * width : (l + 1) * width].reshape(width, 3, width)
        targets = fits_w[l + 1 : l + 4]
        ok = fits_w[l + 2][:, None, None] & (targets & om[l][:, None])[None]
        densities.append(jnp.where(ok, occ, 0))
    band = jnp.stack(bands).astype(bf)
    density = jnp.stack(densities).astype(bf)

    mixed = jnp.einsum("lpmb,lbk->lpmk", three, band, preferred_element_type=f32).astype(bf)
    keep = [tm[t : t + nb] for t in range(3)]

    def pair(t):
        out = jnp.einsum(
            "lmj,lpmc->ljpc",
            density[:, :, t],
            mixed[:, :, :, t * width : (t + 3) * width],
            preferred_element_type=f32,
        )
        ok = jnp.repeat(keep[t], width, axis=1)
        return jnp.where(ok[:, None, None, :], out, 0).astype(bf)

    up = pair(2)
    from_left = shift(up[-1:], "atom", 1)
    down = pair(0)
    from_right = shift(down[:1], "atom", -1)
    mid = pair(1)
    before = jnp.concatenate([from_left, up[:-1]], axis=0)
    after = jnp.concatenate([down[1:], from_right], axis=0)
    sources = jnp.stack([before, mid, after], axis=2)

    def contract(pieces):
        acc = None
        for (lo, hi), piece in zip(bounds, pieces):
            part = jnp.einsum(
                "lrqc,lropc->lqop", piece, sources[:, lo:hi], preferred_element_type=f32
            )
            acc = part if acc is None else acc + part
        return acc

    parts = [contract([piece[s] for piece in both]) for s in range(2)]
    own = jnp.where(side == 0, parts[0], parts[1])
    cross = jnp.where(side == 0, parts[1], parts[0])
    tail = sources[:, low:]
    own = own + jnp.einsum("lrqc,lropc->lqop", rest, tail, preferred_element_type=f32)
    cross = cross + jnp.einsum("lrqc,lropc->lqop", rest_other, tail, preferred_element_type=f32)
    got = shift(cross, "aux", 1)
    sides = jnp.where(
        side == 0,
        jnp.concatenate([own, got], axis=3),
        jnp.concatenate([got, own], axis=3),
    )
    return sides.reshape(nb, aux_local, -1)


def solution(mesh):
    in_specs = (
        P("atom", "aux", None, None),
        P(("atom", "aux"), None),
        P(("atom", "aux"), None),
        P(),
        P(),
        P(),
        P(),
    )
    out_specs = P("atom", "aux", None)
    return jax.shard_map(shards, mesh=mesh, in_specs=in_specs, out_specs=out_specs, check_vma=False)
```
